256 devices in a mesh: slab: 4 (over y), tile: 64 (over x, z, core).
Axes of the slice: x: 4, y: 4, z: 8, core: 2. Of those that a mesh axis runs over, the one named last changes fastest.
Arguments:
- wavefield: float32 [4, 2, 2048, 2048], P(None, None, 'tile'), may hold values from -6 to 6
- slowness: float32 [4, 2048, 2048], P('slab', 'tile'), may hold values from 0.5 to 1
- angular_freq: float32 [4], replicated, may hold values from 1 to 3
- filter_taps: float32 [4, 8, 2], replicated, may hold values from -1.5 to 1.5
Outputs:
- images: float32 [4, 2048, 2048], P('slab', 'tile')
The draws below stay inside these ranges and needn't reach their ends.
All inputs are finite; a program needn't handle non-finite values.
Results may differ from the reference program's by a relative error of at most 0.00002.
Values sent between devices are 32-bit elements; how exact they have to be, the bound alone decides.
No kernel may reach another device: no remote copies, remote signals or barrier semaphores. Data moves between devices by JAX's collectives and lax.ppermute only.
A program may use at most 64 MiB of HBM per device.

```python
import jax
import jax.numpy as jnp

NY = 2048
NF = 4
TERMS = 8
NX = 2048
NZ = 4


def level_of(stream_key, shape, split, least, top_value):
    gain, own = 1.0, jax.random.fold_in(stream_key, 6)
    for dim, blocks in split:
        draws = jnp.exp(jax.random.uniform(jax.random.fold_in(own, dim), (blocks,), jnp.float32, least / len(split), top_value / len(split)))
        gain = gain * jnp.repeat(draws, shape[dim] // blocks).reshape([-1 if axis == dim else 1 for axis in range(len(shape))])
    return gain


def scatter_about(own_key, shape, width, bound, cuts=(), kind=jnp.bfloat16):
    gain = level_of(own_key, shape, cuts, -0.22, 0.18) if cuts else 1.0
    drawn = jax.random.normal(own_key, shape, jnp.float32) * width * gain
    return jnp.minimum(jnp.maximum(drawn, -bound), bound).astype(kind)


def setup_inputs(seed: int = 0) -> dict:
    splits = jax.random.split(jax.random.key(seed), 5)
    return {
        "wavefield": scatter_about(splits[0], (NF, 2, NX, NY), 1.0, 6.0, ((2, 64),), jnp.float32),
        "slowness": jnp.clip(0.5 + 0.5 * jax.random.uniform(splits[1], (NZ, NX, NY), jnp.float32) ** level_of(splits[1], (NZ, NX, NY), ((0, 4), (1, 64)), -0.2, 0.2), 0.5, 1.0),
        "angular_freq": jnp.clip(jax.random.uniform(splits[2], (NF,), jnp.float32, 1.0, 3.0), 1.0, 3.0),
        "filter_taps": scatter_about(splits[3], (NF, TERMS, 2), 0.3, 1.5, (), jnp.float32),
    }


def stencil(padded):
    middle = padded[:, 1:-1, 1:-1]
    beside = padded[:, :-2, 1:-1] + padded[:, 2:, 1:-1] + padded[:, 1:-1, :-2] + padded[:, 1:-1, 2:]
    diagonal = padded[:, :-2, :-2] + padded[:, :-2, 2:] + padded[:, 2:, :-2] + padded[:, 2:, 2:]
    return -0.5 * middle + 0.25 * beside + 0.125 * diagonal


def mcclellan(current, layer_slow):
    padded = jnp.pad(current, ((0, 0), (1, 1), (1, 1)))
    return layer_slow * stencil(padded)


def descend(current, layer_slow, freq_value, taps_here):
    previous = current
    latest = mcclellan(current, layer_slow)
    accum_real = taps_here[0, 0] * previous[0] - taps_here[0, 1] * previous[1]
    accum_imag = taps_here[0, 0] * previous[1] + taps_here[0, 1] * previous[0]
    accum_real = accum_real + taps_here[1, 0] * latest[0] - taps_here[1, 1] * latest[1]
    accum_imag = accum_imag + taps_here[1, 0] * latest[1] + taps_here[1, 1] * latest[0]
    for order_index in range(2, TERMS):
        following = 2.0 * mcclellan(latest, layer_slow) - previous
        previous, latest = latest, following
        accum_real = accum_real + taps_here[order_index, 0] * latest[0] - taps_here[order_index, 1] * latest[1]
        accum_imag = accum_imag + taps_here[order_index, 0] * latest[1] + taps_here[order_index, 1] * latest[0]
    phase_angle = freq_value * layer_slow
    cosine = jnp.cos(phase_angle)
    sine_part = jnp.sin(phase_angle)
    return jnp.stack([accum_real * cosine - accum_imag * sine_part, accum_real * sine_part + accum_imag * cosine])


def reference(wavefield, slowness, angular_freq, filter_taps):
    images = jnp.zeros((NZ, NX, NY), jnp.float32)
    for freq_index in range(NF):
        current = wavefield[freq_index]
        for layer_index in range(NZ):
            current = descend(current, slowness[layer_index], angular_freq[freq_index], filter_taps[freq_index])
            images = images.at[layer_index].add(current[0])
    return images
```

```python
import math

import jax
import jax.numpy as jnp
import numpy as np
from jax import lax
from jax.experimental import pallas as pl
from jax.experimental.pallas import tpu as pltpu
from jax.sharding import PartitionSpec as P

TERMS = 8
DEPTHS = 4
FREQS = 4
LANES = 128
COMPS = 2 * FREQS
HALO = DEPTHS * (TERMS - 1)
ROWS = 32
SPAN = 3 * ROWS
COLS = 512
WIDE = COLS + LANES
BLOCK = 8
VMEM = pl.BlockSpec(memory_space=pltpu.VMEM)
ANY = pl.BlockSpec(memory_space=pl.ANY)
PARAMS = pltpu.CompilerParams(vmem_limit_bytes=48 * 1024 * 1024)


def fit(function, low, high, count):
    angle = (np.arange(400) + 0.5) * np.pi / 400
    q = 0.5 * (low + high) + 0.5 * (high - low) * np.cos(angle)
    rows = np.stack([q**power for power in range(count)], 1)
    return np.linalg.lstsq(rows, function(q), rcond=None)[0]


ARGUMENT_LIMIT = 1.6
SINE = fit(lambda q: np.sin(np.sqrt(q)) / np.sqrt(q), 0.0, ARGUMENT_LIMIT**2, 6)
COSINE = fit(lambda q: np.cos(np.sqrt(q)), 0.0, ARGUMENT_LIMIT**2, 6)


def edge_columns(load, block):
    last = 2048 // COLS - 1
    right = load(pl.multiple_of(jnp.minimum(block + 1, last) * COLS, LANES))
    left = load(pl.multiple_of(jnp.maximum(block * COLS - LANES, 0), LANES))
    right = jnp.where(block < last, right, 0.0)
    left = jnp.where(block > 0, left, 0.0)
    lane = lax.broadcasted_iota(jnp.int32, right.shape, right.ndim - 1)
    return jnp.where(lane < LANES // 2, right, left)


def pack_kernel(wave_ref, slow_ref, head_ref, tail_ref, *slow_out):
    here = lax.axis_index("slab")
    start = pl.multiple_of(here * COLS, COLS)

    def put(rows, lanes):
        turned = jnp.swapaxes(rows, 0, 1)
        return turned

    for group in range(ROWS // 8):
        for piece in range(WIDE // LANES):
            parts = []
            for comp in range(2):
                for freq in range(FREQS):
                    source = wave_ref.at[freq, comp, group * 8 : group * 8 + 8]
                    if piece < COLS // LANES:
                        parts.append(source[:, pl.ds(start + piece * LANES, LANES)])
                    else:
                        parts.append(edge_columns(lambda at: source[:, pl.ds(at, LANES)], here))
            turned = put(jnp.stack(parts), None)
            lanes = slice(piece * LANES, (piece + 1) * LANES)
            low = group * 8
            keep = min(low + 8, HALO) - low
            head_ref[low : low + keep, :, lanes] = turned[:keep]
            skip = max(ROWS - HALO - low, 0)
            tail_ref[low + skip - (ROWS - HALO) : low + 8 - (ROWS - HALO), :, lanes] = turned[skip:]
    for shift, out in enumerate(slow_out):
        block = lax.rem(here + shift, DEPTHS)
        out[:, :COLS] = slow_ref[0, :, pl.ds(pl.multiple_of(block * COLS, COLS), COLS)]
        out[:, COLS:] = edge_columns(lambda at: slow_ref[0, :, pl.ds(at, LANES)], block)


def edge_kernel(*refs):
    pieces, (first_ref, last_ref, stacked) = refs[:DEPTHS], refs[DEPTHS:]
    here = lax.axis_index("slab")
    for shift, piece in enumerate(pieces):
        stacked[lax.rem(here - shift + DEPTHS, DEPTHS)] = piece[...]
    low = 0
    for depth in range(DEPTHS):
        count = ROWS - 8 * depth
        first_ref[low : low + count] = stacked[depth, :count]
        last_ref[low : low + count] = stacked[depth, ROWS - count :]
        low += count


def main_kernel(head, tail, above, below, *refs):
    pieces, (edge_above, edge_below, omega, taps, image, terms, slow, wide, sems) = (
        refs[:DEPTHS],
        refs[DEPTHS:],
    )
    here = lax.axis_index("slab")
    copies = []

    def bring(source, target):
        copy = pltpu.make_async_copy(source, target, sems.at[len(copies)])
        copy.start()
        copies.append(copy)

    begin = ROWS - HALO
    bring(above, terms.at[0, begin:ROWS])
    bring(head, terms.at[0, ROWS : ROWS + HALO])
    bring(tail.at[HALO - begin :], terms.at[0, ROWS + HALO : 2 * ROWS])
    bring(below, terms.at[0, 2 * ROWS : 2 * ROWS + HALO])
    for shift, piece in enumerate(pieces):
        bring(piece, slow.at[lax.rem(here - shift + DEPTHS, DEPTHS), ROWS : 2 * ROWS])
    low = 0
    for depth in range(DEPTHS):
        count = ROWS - 8 * depth
        bring(edge_above.at[low : low + count], slow.at[depth, ROWS - count : ROWS])
        bring(edge_below.at[low : low + count], slow.at[depth, 2 * ROWS : 2 * ROWS + count])
        low += count
    for copy in copies:
        copy.wait()

    sublane = lax.broadcasted_iota(jnp.int32, (COMPS, LANES), 0)
    real = sublane < FREQS

    def coefficient(index):
        return jnp.where(real, -float(SINE[index]), float(COSINE[index])).astype(jnp.float32)

    def rows_loop(low, high, body):
        count = high - low
        full = count // BLOCK

        def step(index, carry):
            body(low + index * BLOCK, BLOCK)
            return carry

        lax.fori_loop(0, full, step, 0)
        if count % BLOCK:
            body(low + full * BLOCK, count % BLOCK)

    for depth in range(DEPTHS):
        reach = HALO - depth * (TERMS - 1)
        lower, upper = ROWS - reach, 2 * ROWS + reach

        def spread(start, count):
            for row in range(count):
                line = slow[depth, pl.ds(start + row, 1), :] * 2.0
                wide[start + row] = jnp.broadcast_to(line, (COMPS, WIDE))

        rows_loop(lower + 1, upper - 1, spread)
        for order in range(1, TERMS):

            def apply(start, count):
                source = terms[order - 1, pl.ds(start - 1, count + 2)]
                pairs = source[:-1] + source[1:]
                tall = pairs[:-1] + pairs[1:]
                beside = tall + pltpu.roll(tall, 1, 2)
                full = beside + pltpu.roll(beside, WIDE - 1, 2)
                fresh = wide[pl.ds(start, count)] * (0.125 * full - source[1:-1])
                if order == 1:
                    fresh = 0.5 * fresh
                else:
                    fresh = fresh - terms[order - 2, pl.ds(start, count)]
                terms[order, pl.ds(start, count)] = fresh

            rows_loop(lower + order, upper - order, apply)

        def finish(start, count):
            for piece in range(WIDE // LANES):
                lanes = slice(piece * LANES, (piece + 1) * LANES)
                straight, crossed = None, None
                for order in range(TERMS):
                    term = terms[order, pl.ds(start, count), :, lanes]
                    one, other = taps[order] * term, taps[TERMS + order] * term
                    straight = one if straight is None else straight + one
                    crossed = other if crossed is None else crossed + other
                filtered = straight + pltpu.roll(crossed, FREQS, 1)
                offset = omega[...] * wide[pl.ds(start, count), :, lanes] - math.pi / 2
                square = offset * offset
                poly = coefficient(5)
                for index in range(4, -1, -1):
                    poly = poly * square + coefficient(index)
                own = poly * jnp.where(real, offset, 1.0)
                other = pltpu.roll(own, FREQS, 1)
                cosine = jnp.where(real, own, other)
                sine = jnp.where(real, -other, own)
                terms[0, pl.ds(start, count), :, lanes] = (
                    filtered * cosine + pltpu.roll(filtered, FREQS, 1) * sine
                )

        rows_loop(lower + TERMS - 1, upper - TERMS + 1, finish)

        def gather(index, carry):
            start = pl.multiple_of(index * 8, 8)
            block = terms[0, pl.ds(ROWS + start, 8), :, :COLS]
            image[depth, pl.ds(start, 8)] = jnp.sum(block[:, :FREQS], axis=1)
            return carry

        lax.fori_loop(0, ROWS // 8, gather, 0)


def local(wavefield, slowness, angular_freq, filter_taps):
    tiles, slabs = lax.axis_size("tile"), lax.axis_size("slab")
    shape = jax.ShapeDtypeStruct
    f32 = jnp.float32
    packed = pl.pallas_call(
        pack_kernel,
        out_shape=[shape((HALO, COMPS, WIDE), f32)] * 2 + [shape((ROWS, WIDE), f32)] * DEPTHS,
        in_specs=[VMEM] * 2,
        out_specs=[VMEM] * (2 + DEPTHS),
        compiler_params=PARAMS,
        name="pack",
    )(wavefield, slowness)
    head, tail, pieces = packed[0], packed[1], packed[2:]
    up = [(i + 1, i) for i in range(tiles - 1)]
    down = [(i, i + 1) for i in range(tiles - 1)]
    pieces = [pieces[0]] + [
        lax.ppermute(pieces[k], "slab", [(i, (i + k) % slabs) for i in range(slabs)])
        for k in range(1, slabs)
    ]
    below = lax.ppermute(head, "tile", up)
    above = lax.ppermute(tail, "tile", down)
    edge_rows = sum(ROWS - 8 * depth for depth in range(DEPTHS))
    first, last = pl.pallas_call(
        edge_kernel,
        out_shape=[shape((edge_rows, WIDE), f32)] * 2,
        in_specs=[VMEM] * DEPTHS,
        out_specs=[VMEM] * 2,
        scratch_shapes=[pltpu.VMEM((DEPTHS, ROWS, WIDE), f32)],
        compiler_params=PARAMS,
        name="edges",
    )(*pieces)
    edge_below = lax.ppermute(first, "tile", up)
    edge_above = lax.ppermute(last, "tile", down)

    omega = jnp.tile(0.5 * angular_freq, 2)[:, None] * jnp.ones((1, LANES), f32)
    real, imag = filter_taps[:, :, 0].T, filter_taps[:, :, 1].T
    straight = jnp.concatenate([real, real], axis=1)
    crossed = jnp.concatenate([imag, -imag], axis=1)
    taps = jnp.concatenate([straight, crossed], axis=0)[:, :, None] * jnp.ones((1, 1, LANES), f32)

    image = pl.pallas_call(
        main_kernel,
        out_shape=shape((DEPTHS, ROWS, COLS), f32),
        in_specs=[ANY] * (4 + DEPTHS + 2) + [VMEM] * 2,
        out_specs=VMEM,
        scratch_shapes=[
            pltpu.VMEM((TERMS, SPAN, COMPS, WIDE), f32),
            pltpu.VMEM((DEPTHS, SPAN, WIDE), f32),
            pltpu.VMEM((SPAN, COMPS, WIDE), f32),
            pltpu.SemaphoreType.DMA((4 + 3 * DEPTHS,)),
        ],
        compiler_params=PARAMS,
        name="migrate",
    )(head, tail, above, below, *pieces, edge_above, edge_below, omega, taps)
    return lax.all_to_all(image, "slab", 0, 2, tiled=True)


def solution(mesh):
    placed = (P(None, None, "tile", None), P("slab", "tile", None), P(), P())
    return jax.shard_map(
        local, mesh=mesh, in_specs=placed, out_specs=P("slab", "tile", None), check_vma=False
    )
```

```python
import math

import jax
import jax.numpy as jnp
import numpy as np
from jax import lax
from jax.experimental import pallas as pl
from jax.experimental.pallas import tpu as pltpu
from jax.sharding import PartitionSpec as P

TERMS = 8
DEPTHS = 4
FREQS = 4
LANES = 128
COMPS = 2 * FREQS
HALO = DEPTHS * (TERMS - 1)
ROWS = 32
SPAN = 3 * ROWS
COLS = 512
WIDE = COLS + LANES
APPLY = 16
FINISH = 4
SPREAD = 8
VMEM = pl.BlockSpec(memory_space=pltpu.VMEM)
ANY = pl.BlockSpec(memory_space=pl.ANY)
PARAMS = pltpu.CompilerParams(vmem_limit_bytes=48 * 1024 * 1024)

SCRATCH = [
    pltpu.VMEM((DEPTHS, SPAN, WIDE), jnp.float32),
    pltpu.VMEM((SPAN, COMPS, WIDE), jnp.float32),
    pltpu.VMEM((DEPTHS * ROWS, WIDE), jnp.float32),
    pltpu.SemaphoreType.DMA((4 + 3 * DEPTHS,)),
] + [pltpu.VMEM((SPAN, COMPS, WIDE), jnp.float32)] * TERMS


def fit(function, low, high, count):
    angle = (np.arange(400) + 0.5) * np.pi / 400
    q = 0.5 * (low + high) + 0.5 * (high - low) * np.cos(angle)
    rows = np.stack([q**power for power in range(count)], 1)
    return np.linalg.lstsq(rows, function(q), rcond=None)[0]


ARGUMENT_LIMIT = 1.6
SINE = fit(lambda q: np.sin(np.sqrt(q)) / np.sqrt(q), 0.0, ARGUMENT_LIMIT**2, 6)
COSINE = fit(lambda q: np.cos(np.sqrt(q)), 0.0, ARGUMENT_LIMIT**2, 6)


def edge_columns(load, block):
    last = 2048 // COLS - 1
    right = load(pl.multiple_of(jnp.minimum(block + 1, last) * COLS, LANES))
    left = load(pl.multiple_of(jnp.maximum(block * COLS - LANES, 0), LANES))
    right = jnp.where(block < last, right, 0.0)
    left = jnp.where(block > 0, left, 0.0)
    lane = lax.broadcasted_iota(jnp.int32, right.shape, right.ndim - 1)
    return jnp.where(lane < LANES // 2, right, left)


def shuffle(column_axis):
    vectors = WIDE // LANES
    column = lax.broadcasted_iota(jnp.int32, (WIDE, WIDE), column_axis)
    place = lax.broadcasted_iota(jnp.int32, (WIDE, WIDE), 1 - column_axis)
    lane = place & (LANES - 1)
    here = lane * vectors + (place >> 7)
    return jnp.where(column == here, 1.0, 0.0).astype(jnp.bfloat16)


def exact_dot(rows, matrix):
    high = rows.astype(jnp.bfloat16)
    rest = rows - high.astype(jnp.float32)
    middle = rest.astype(jnp.bfloat16)
    low = (rest - middle.astype(jnp.float32)).astype(jnp.bfloat16)
    dots = [jnp.dot(part, matrix, preferred_element_type=jnp.float32) for part in (high, middle, low)]
    return (dots[0] + dots[1]) + dots[2]


def pack_kernel(wave_ref, slow_ref, head_ref, tail_ref, *refs):
    slow_out, lined = refs[:DEPTHS], refs[DEPTHS]
    here = lax.axis_index("slab")
    start = pl.multiple_of(here * COLS, COLS)
    for group in range(ROWS // 8):
        for piece in range(WIDE // LANES):
            parts = []
            for comp in range(2):
                for freq in range(FREQS):
                    source = wave_ref.at[freq, comp, group * 8 : group * 8 + 8]
                    if piece < COLS // LANES:
                        parts.append(source[:, pl.ds(start + piece * LANES, LANES)])
                    else:
                        parts.append(edge_columns(lambda at: source[:, pl.ds(at, LANES)], here))
            turned = jnp.swapaxes(jnp.stack(parts), 0, 1).reshape(8 * COMPS, LANES)
            low = group * 8 * COMPS
            lined[low : low + 8 * COMPS, piece * LANES : (piece + 1) * LANES] = turned
    for shift in range(DEPTHS):
        block = lax.rem(here + shift, DEPTHS)
        low = ROWS * COMPS + shift * ROWS
        lined[low : low + ROWS, :COLS] = slow_ref[
            0, :, pl.ds(pl.multiple_of(block * COLS, COLS), COLS)
        ]
        lined[low : low + ROWS, COLS:] = edge_columns(lambda at: slow_ref[0, :, pl.ds(at, LANES)], block)
    lined[...] = exact_dot(lined[...], shuffle(0))
    field = lined[: ROWS * COMPS].reshape(ROWS, COMPS, WIDE)
    head_ref[...] = field[:HALO]
    tail_ref[...] = field[ROWS - HALO :]
    for shift, out in enumerate(slow_out):
        low = ROWS * COMPS + shift * ROWS
        out[...] = lined[low : low + ROWS]


def edge_kernel(*refs):
    pieces, (first_ref, last_ref, stacked) = refs[:DEPTHS], refs[DEPTHS:]
    here = lax.axis_index("slab")
    for shift, piece in enumerate(pieces):
        stacked[lax.rem(here - shift + DEPTHS, DEPTHS)] = piece[...]
    low = 0
    for depth in range(DEPTHS):
        count = ROWS - 8 * depth
        first_ref[low : low + count] = stacked[depth, :count]
        last_ref[low : low + count] = stacked[depth, ROWS - count :]
        low += count


def main_kernel(head, tail, above, below, *refs):
    pieces, (edge_above, edge_below, omega, taps, image, slow, wide, mixed, sems, *terms) = (
        refs[:DEPTHS],
        refs[DEPTHS:],
    )
    here = lax.axis_index("slab")
    copies = []

    def bring(source, target):
        copy = pltpu.make_async_copy(source, target, sems.at[len(copies)])
        copy.start()
        copies.append(copy)

    begin = ROWS - HALO
    bring(above, terms[0].at[begin:ROWS])
    bring(head, terms[0].at[ROWS : ROWS + HALO])
    bring(tail.at[HALO - begin :], terms[0].at[ROWS + HALO : 2 * ROWS])
    bring(below, terms[0].at[2 * ROWS : 2 * ROWS + HALO])
    for shift, piece in enumerate(pieces):
        bring(piece, slow.at[lax.rem(here - shift + DEPTHS, DEPTHS), ROWS : 2 * ROWS])
    low = 0
    for depth in range(DEPTHS):
        count = ROWS - 8 * depth
        bring(edge_above.at[low : low + count], slow.at[depth, ROWS - count : ROWS])
        bring(edge_below.at[low : low + count], slow.at[depth, 2 * ROWS : 2 * ROWS + count])
        low += count
    for copy in copies:
        copy.wait()

    sublane = lax.broadcasted_iota(jnp.int32, (COMPS, LANES), 0)
    real = sublane < FREQS

    def coefficient(index):
        return jnp.where(real, -float(SINE[index]), float(COSINE[index])).astype(jnp.float32)

    def rows_loop(low, high, size, body):
        full = (high - low) // size

        def step(index, carry):
            body(low + index * size, size)
            return carry

        lax.fori_loop(0, full, step, 0)
        if (high - low) % size:
            body(low + full * size, (high - low) % size)

    def covering_loop(low, high, size, body):

        def step(index, carry):
            body(jnp.minimum(low + index * size, high - size), size)
            return carry

        lax.fori_loop(0, -(-(high - low) // size), step, 0)

    for depth in range(DEPTHS):
        reach = HALO - depth * (TERMS - 1)
        lower, upper = ROWS - reach, 2 * ROWS + reach

        def spread(start, count):
            for row in range(count):
                line = slow[depth, pl.ds(start + row, 1), :] * 2.0
                wide[start + row] = jnp.broadcast_to(line, (COMPS, WIDE))

        covering_loop(lower + 1, upper - 1, SPREAD, spread)
        for order in range(1, TERMS):

            def apply(start, count):
                pieces = range(WIDE // LANES)

                def load(ref, at):
                    return [ref[at, :, p * LANES : (p + 1) * LANES] for p in pieces]

                here_row = load(terms[order - 1], start)
                pair = [a + b for a, b in zip(load(terms[order - 1], start - 1), here_row)]
                for row in range(count):
                    next_row = load(terms[order - 1], start + row + 1)
                    next_pair = [a + b for a, b in zip(here_row, next_row)]
                    tall = [a + b for a, b in zip(pair, next_pair)]
                    before = pltpu.roll(tall[-1], 1, 1)
                    after = pltpu.roll(tall[0], LANES - 1, 1)
                    chain = [before] + tall + [after]
                    sums = [a + b for a, b in zip(chain[:-1], chain[1:])]
                    full = [a + b for a, b in zip(sums[:-1], sums[1:])]
                    for p in pieces:
                        lanes = slice(p * LANES, (p + 1) * LANES)
                        fresh = wide[start + row, :, lanes] * (0.125 * full[p] - here_row[p])
                        if order == 1:
                            fresh = 0.5 * fresh
                        else:
                            fresh = fresh - terms[order - 2][start + row, :, lanes]
                        terms[order][start + row, :, lanes] = fresh
                    here_row, pair = next_row, next_pair

            covering_loop(lower + order, upper - order, APPLY, apply)

        def finish(start, count):
            for row in range(count):
                for piece in range(WIDE // LANES):
                    lanes = slice(piece * LANES, (piece + 1) * LANES)
                    straight, crossed = None, None
                    for order in range(TERMS):
                        term = terms[order][start + row, :, lanes]
                        one, other = taps[order] * term, taps[TERMS + order] * term
                        straight = one if straight is None else straight + one
                        crossed = other if crossed is None else crossed + other
                    filtered = straight + pltpu.roll(crossed, FREQS, 0)
                    offset = omega[...] * wide[start + row, :, lanes] - math.pi / 2
                    square = offset * offset
                    poly = coefficient(5)
                    for index in range(4, -1, -1):
                        poly = poly * square + coefficient(index)
                    own = poly * jnp.where(real, offset, 1.0)
                    other = pltpu.roll(own, FREQS, 0)
                    cosine = jnp.where(real, own, other)
                    sine = jnp.where(real, -other, own)
                    terms[0][start + row, :, lanes] = (
                        filtered * cosine + pltpu.roll(filtered, FREQS, 0) * sine
                    )

        rows_loop(lower + TERMS - 1, upper - TERMS + 1, FINISH, finish)

        def gather(index, carry):
            start = pl.multiple_of(index * 8, 8)
            block = terms[0][pl.ds(ROWS + start, 8)]
            mixed[pl.ds(depth * ROWS + start, 8)] = jnp.sum(block[:, :FREQS], axis=1)
            return carry

        lax.fori_loop(0, ROWS // 8, gather, 0)
    image[...] = exact_dot(mixed[...], shuffle(1)[:, :COLS]).reshape(image.shape)


def local(wavefield, slowness, angular_freq, filter_taps):
    tiles, slabs = lax.axis_size("tile"), lax.axis_size("slab")
    shape = jax.ShapeDtypeStruct
    f32 = jnp.float32
    packed = pl.pallas_call(
        pack_kernel,
        out_shape=[shape((HALO, COMPS, WIDE), f32)] * 2 + [shape((ROWS, WIDE), f32)] * DEPTHS,
        in_specs=[VMEM] * 2,
        out_specs=[VMEM] * (2 + DEPTHS),
        scratch_shapes=[pltpu.VMEM((ROWS * COMPS + DEPTHS * ROWS, WIDE), f32)],
        compiler_params=PARAMS,
        name="pack",
    )(wavefield, slowness)
    head, tail, pieces = packed[0], packed[1], packed[2:]
    up = [(i + 1, i) for i in range(tiles - 1)]
    down = [(i, i + 1) for i in range(tiles - 1)]
    pieces = [pieces[0]] + [
        lax.ppermute(pieces[k], "slab", [(i, (i + k) % slabs) for i in range(slabs)])
        for k in range(1, slabs)
    ]
    below = lax.ppermute(head, "tile", up)
    above = lax.ppermute(tail, "tile", down)
    edge_rows = sum(ROWS - 8 * depth for depth in range(DEPTHS))
    first, last = pl.pallas_call(
        edge_kernel,
        out_shape=[shape((edge_rows, WIDE), f32)] * 2,
        in_specs=[VMEM] * DEPTHS,
        out_specs=[VMEM] * 2,
        scratch_shapes=[pltpu.VMEM((DEPTHS, ROWS, WIDE), f32)],
        compiler_params=PARAMS,
        name="edges",
    )(*pieces)
    edge_below = lax.ppermute(first, "tile", up)
    edge_above = lax.ppermute(last, "tile", down)

    omega = jnp.tile(0.5 * angular_freq, 2)[:, None] * jnp.ones((1, LANES), f32)
    real, imag = filter_taps[:, :, 0].T, filter_taps[:, :, 1].T
    straight = jnp.concatenate([real, real], axis=1)
    crossed = jnp.concatenate([imag, -imag], axis=1)
    taps = jnp.concatenate([straight, crossed], axis=0)[:, :, None] * jnp.ones((1, 1, LANES), f32)

    image = pl.pallas_call(
        main_kernel,
        out_shape=shape((DEPTHS, ROWS, COLS), f32),
        in_specs=[ANY] * (4 + DEPTHS + 2) + [VMEM] * 2,
        out_specs=VMEM,
        scratch_shapes=SCRATCH,
        compiler_params=PARAMS,
        name="migrate",
    )(head, tail, above, below, *pieces, edge_above, edge_below, omega, taps)
    return lax.all_to_all(image, "slab", 0, 2, tiled=True)


def solution(mesh):
    placed = (P(None, None, "tile", None), P("slab", "tile", None), P(), P())
    return jax.shard_map(
        local, mesh=mesh, in_specs=placed, out_specs=P("slab", "tile", None), check_vma=False
    )
```

```python
import math

import jax
import jax.numpy as jnp
import numpy as np
from jax import lax
from jax.experimental import pallas as pl
from jax.experimental.pallas import tpu as pltpu
from jax.sharding import PartitionSpec as P

TERMS = 8
DEPTHS = 4
FREQS = 4
LANES = 128
COMPS = 2 * FREQS
HALO = DEPTHS * (TERMS - 1)
ROWS = 32
SPAN = 3 * ROWS
GRID = 2048
COLS = 512
WIDE = COLS + LANES
MOST = 20
FINISH = 8
SPREAD = 8
VMEM = pl.BlockSpec(memory_space=pltpu.VMEM)
ANY = pl.BlockSpec(memory_space=pl.ANY)
HBM = pl.BlockSpec(memory_space=pltpu.HBM)
SMEM = pl.BlockSpec(memory_space=pltpu.SMEM)
PARAMS = pltpu.CompilerParams(vmem_limit_bytes=48 * 1024 * 1024)

SCRATCH = [
    pltpu.VMEM((DEPTHS, SPAN, WIDE), jnp.float32),
    pltpu.VMEM((SPAN, COMPS, WIDE), jnp.float32),
    pltpu.VMEM((DEPTHS * ROWS, WIDE), jnp.float32),
    pltpu.VMEM((DEPTHS, ROWS, COLS), jnp.float32),
    pltpu.VMEM((2 * TERMS, COMPS, LANES), jnp.float32),
    pltpu.SemaphoreType.DMA((5 + 2 * DEPTHS,)),
] + [pltpu.VMEM((SPAN, COMPS, WIDE), jnp.float32)] * TERMS


def fit(function, low, high, count):
    angle = (np.arange(400) + 0.5) * np.pi / 400
    q = 0.5 * (low + high) + 0.5 * (high - low) * np.cos(angle)
    rows = np.stack([q**power for power in range(count)], 1)
    return np.linalg.lstsq(rows, function(q), rcond=None)[0]


COEFFICIENTS = 6
ARGUMENT_LIMIT = 1.5
SINE = fit(lambda q: np.sin(np.sqrt(q)) / np.sqrt(q), 0.0, ARGUMENT_LIMIT**2, COEFFICIENTS)
COSINE = fit(lambda q: np.cos(np.sqrt(q)), 0.0, ARGUMENT_LIMIT**2, COEFFICIENTS)


def edge_columns(right, left, block):
    right = jnp.where(block < GRID // COLS - 1, right, 0.0)
    left = jnp.where(block > 0, left, 0.0)
    lane = lax.broadcasted_iota(jnp.int32, right.shape, right.ndim - 1)
    return jnp.where(lane < LANES // 2, right, left)


def edge_starts(block):
    right = jnp.minimum(block + 1, GRID // COLS - 1) * COLS
    left = jnp.maximum(block * COLS - LANES, 0)
    return pl.multiple_of(right, LANES), pl.multiple_of(left, LANES)


def shuffle(column_axis):
    vectors = WIDE // LANES
    column = lax.broadcasted_iota(jnp.int32, (WIDE, WIDE), column_axis)
    place = lax.broadcasted_iota(jnp.int32, (WIDE, WIDE), 1 - column_axis)
    lane = place & (LANES - 1)
    here = lane * vectors + (place >> 7)
    return jnp.where(column == here, 1.0, 0.0).astype(jnp.bfloat16)


def exact_dot(rows, matrix):
    high = rows.astype(jnp.bfloat16)
    rest = rows - high.astype(jnp.float32)
    middle = rest.astype(jnp.bfloat16)
    low = (rest - middle.astype(jnp.float32)).astype(jnp.bfloat16)
    dots = [jnp.dot(part, matrix, preferred_element_type=jnp.float32) for part in (high, middle, low)]
    return (dots[0] + dots[1]) + dots[2]


def slow_kernel(slow_ref, *refs):
    pieces, (held, sem) = refs[:DEPTHS], refs[DEPTHS:]
    here = lax.axis_index("slab")
    copy = pltpu.make_async_copy(slow_ref.at[0], held, sem)
    copy.start()
    copy.wait()
    for shift, out in enumerate(pieces):
        block = lax.rem(here + shift, DEPTHS)
        right, left = edge_starts(block)
        out[:, :COLS] = held[:, pl.ds(pl.multiple_of(block * COLS, COLS), COLS)]
        out[:, COLS:] = edge_columns(held[:, pl.ds(right, LANES)], held[:, pl.ds(left, LANES)], block)


def wave_kernel(wave_ref, head_ref, tail_ref, held, edges, lined, sems):
    here = lax.axis_index("slab")
    right, left = edge_starts(here)
    start = pl.multiple_of(here * COLS, COLS)
    copies = [
        pltpu.make_async_copy(wave_ref.at[:, :, :, pl.ds(start, COLS)], held, sems.at[0]),
        pltpu.make_async_copy(wave_ref.at[:, :, :, pl.ds(right, LANES)], edges.at[0], sems.at[1]),
        pltpu.make_async_copy(wave_ref.at[:, :, :, pl.ds(left, LANES)], edges.at[1], sems.at[2]),
    ]
    for copy in copies:
        copy.start()
    matrix = shuffle(0)
    for copy in copies:
        copy.wait()
    for group in range(ROWS // 8):
        rows = slice(group * 8, group * 8 + 8)
        for piece in range(WIDE // LANES):
            lanes = slice(piece * LANES, (piece + 1) * LANES)
            parts = []
            for comp in range(2):
                for freq in range(FREQS):
                    if piece < COLS // LANES:
                        parts.append(held[freq, comp, rows, lanes])
                    else:
                        parts.append(
                            edge_columns(edges[0, freq, comp, rows], edges[1, freq, comp, rows], here)
                        )
            turned = jnp.swapaxes(jnp.stack(parts), 0, 1).reshape(8 * COMPS, LANES)
            low = group * 8 * COMPS
            lined[low : low + 8 * COMPS, lanes] = turned
    field = exact_dot(lined[...], matrix).reshape(ROWS, COMPS, WIDE)
    head_ref[...] = field[:HALO]
    tail_ref[...] = field[ROWS - HALO :]


def edge_kernel(*refs):
    pieces, (own_ref, first_ref, last_ref, lined) = refs[:DEPTHS], refs[DEPTHS:]
    here = lax.axis_index("slab")
    for shift, piece in enumerate(pieces):
        depth = lax.rem(here - shift + DEPTHS, DEPTHS)
        lined[pl.ds(pl.multiple_of(depth * ROWS, ROWS), ROWS)] = piece[...]
    own = exact_dot(lined[...], shuffle(0)).reshape(DEPTHS, ROWS, WIDE)
    own_ref[...] = own
    low = 0
    for depth in range(DEPTHS):
        count = ROWS - 8 * depth
        first_ref[low : low + count] = own[depth, :count]
        last_ref[low : low + count] = own[depth, ROWS - count :]
        low += count


def block_rows(count):
    return min(range(8, MOST + 1), key=lambda size: -(-count // size) * (size + 8))


def main_kernel(
    head, tail, above, below, own, edge_above, edge_below, omega_ref, taps_ref, *refs
):
    images, (slow, wide, mixed, held, taps, sems, *terms) = refs[:DEPTHS], refs[DEPTHS:]
    here = lax.axis_index("slab")
    copies = []

    def bring(source, target):
        copy = pltpu.make_async_copy(source, target, sems.at[len(copies)])
        copy.start()
        copies.append(copy)

    begin = ROWS - HALO
    bring(above, terms[0].at[begin:ROWS])
    bring(head, terms[0].at[ROWS : ROWS + HALO])
    bring(tail.at[HALO - begin :], terms[0].at[ROWS + HALO : 2 * ROWS])
    bring(below, terms[0].at[2 * ROWS : 2 * ROWS + HALO])
    bring(own, slow.at[:, ROWS : 2 * ROWS])
    low = 0
    for depth in range(DEPTHS):
        count = ROWS - 8 * depth
        bring(edge_above.at[low : low + count], slow.at[depth, ROWS - count : ROWS])
        bring(edge_below.at[low : low + count], slow.at[depth, 2 * ROWS : 2 * ROWS + count])
        low += count
    matrix = shuffle(1)[:, :COLS]
    sublane = lax.broadcasted_iota(jnp.int32, (COMPS, LANES), 0)
    real = sublane < FREQS

    def of_frequency(value):
        vector = jnp.full((COMPS, LANES), value(FREQS - 1), jnp.float32)
        for freq in range(FREQS - 1):
            vector = jnp.where((sublane & (FREQS - 1)) == freq, value(freq), vector)
        return vector

    def tap(part, order):
        return of_frequency(lambda freq: taps_ref[(freq * TERMS + order) * 2 + part])

    omega = of_frequency(lambda freq: 0.5 * omega_ref[freq])
    straight_taps = [tap(0, order) for order in range(TERMS)]
    crossed_taps = [jnp.where(real, tap(1, order), -tap(1, order)) for order in range(TERMS)]
    for order in range(TERMS):
        taps[order] = straight_taps[order]
        taps[TERMS + order] = crossed_taps[order]

    for copy in copies[4:]:
        copy.wait()

    def coefficient(index):
        return jnp.where(real, -float(SINE[index]), float(COSINE[index])).astype(jnp.float32)

    def rows_loop(low, high, size, body):
        full = (high - low) // size

        def step(index, carry):
            body(low + index * size, size)
            return carry

        lax.fori_loop(0, full, step, 0)
        if (high - low) % size:
            body(low + full * size, (high - low) % size)

    def covering_loop(low, high, size, body):

        def step(index, carry):
            body(jnp.minimum(low + index * size, high - size), size)
            return carry

        lax.fori_loop(0, -(-(high - low) // size), step, 0)

    for depth in range(DEPTHS):
        reach = HALO - depth * (TERMS - 1)
        lower, upper = ROWS - reach, 2 * ROWS + reach

        def spread(start, count):
            for row in range(count):
                line = slow[depth, pl.ds(start + row, 1), :] * 2.0
                wide[start + row] = jnp.broadcast_to(line, (COMPS, WIDE))

        covering_loop(lower + 1, upper - 1, SPREAD, spread)
        if depth == 0:
            for copy in copies[:4]:
                copy.wait()
        for order in range(1, TERMS):

            def apply(start, count):
                pieces = range(WIDE // LANES)

                def load(ref, at):
                    return [ref[at, :, p * LANES : (p + 1) * LANES] for p in pieces]

                here_row = load(terms[order - 1], start)
                pair = [a + b for a, b in zip(load(terms[order - 1], start - 1), here_row)]
                for row in range(count):
                    next_row = load(terms[order - 1], start + row + 1)
                    next_pair = [a + b for a, b in zip(here_row, next_row)]
                    tall = [a + b for a, b in zip(pair, next_pair)]
                    before = pltpu.roll(tall[-1], 1, 1)
                    after = pltpu.roll(tall[0], LANES - 1, 1)
                    chain = [before] + tall + [after]
                    sums = [a + b for a, b in zip(chain[:-1], chain[1:])]
                    full = [a + b for a, b in zip(sums[:-1], sums[1:])]
                    for p in pieces:
                        lanes = slice(p * LANES, (p + 1) * LANES)
                        fresh = wide[start + row, :, lanes] * (0.125 * full[p] - here_row[p])
                        if order == 1:
                            fresh = 0.5 * fresh
                        else:
                            fresh = fresh - terms[order - 2][start + row, :, lanes]
                        terms[order][start + row, :, lanes] = fresh
                    here_row, pair = next_row, next_pair

            covering_loop(lower + order, upper - order, block_rows(upper - lower - 2 * order), apply)

        def finish(start, count):
            rows = range(count)
            for piece in range(WIDE // LANES):
                lanes = slice(piece * LANES, (piece + 1) * LANES)
                straight, crossed = [None] * count, [None] * count
                for order in range(TERMS):
                    one, other = taps[order], taps[TERMS + order]
                    for row in rows:
                        term = terms[order][start + row, :, lanes]
                        along, across = one * term, other * term
                        straight[row] = along if order == 0 else straight[row] + along
                        crossed[row] = across if order == 0 else crossed[row] + across
                offsets = [omega * wide[start + row, :, lanes] - math.pi / 2 for row in rows]
                squares = [offset * offset for offset in offsets]
                polys = [coefficient(COEFFICIENTS - 1)] * count
                for index in range(COEFFICIENTS - 2, -1, -1):
                    polys = [poly * square + coefficient(index) for poly, square in zip(polys, squares)]
                for row in rows:
                    filtered = straight[row] + pltpu.roll(crossed[row], FREQS, 0)
                    own = polys[row] * jnp.where(real, offsets[row], 1.0)
                    other = pltpu.roll(own, FREQS, 0)
                    cosine = jnp.where(real, own, other)
                    sine = jnp.where(real, -other, own)
                    terms[0][start + row, :, lanes] = (
                        filtered * cosine + pltpu.roll(filtered, FREQS, 0) * sine
                    )

        rows_loop(lower + TERMS - 1, upper - TERMS + 1, FINISH, finish)

        def gather(index, carry):
            start = pl.multiple_of(index * 8, 8)
            block = terms[0][pl.ds(ROWS + start, 8)]
            mixed[pl.ds(depth * ROWS + start, 8)] = jnp.sum(block[:, :FREQS], axis=1)
            return carry

        lax.fori_loop(0, ROWS // 8, gather, 0)
    held[...] = exact_dot(mixed[...], matrix).reshape(held.shape)
    for shift, image in enumerate(images):
        image[...] = held[lax.rem(here + shift, DEPTHS)]


def join_kernel(*refs):
    pieces, (out, sems) = refs[:DEPTHS], refs[DEPTHS:]
    here = lax.axis_index("slab")
    copies = []
    for shift, piece in enumerate(pieces):
        block = lax.rem(here - shift + DEPTHS, DEPTHS)
        columns = pl.ds(pl.multiple_of(block * COLS, COLS), COLS)
        copies.append(pltpu.make_async_copy(piece, out.at[0, :, columns], sems.at[shift]))
        copies[-1].start()
    for copy in copies:
        copy.wait()


def local(wavefield, slowness, angular_freq, filter_taps):
    tiles, slabs = lax.axis_size("tile"), lax.axis_size("slab")
    f32 = jnp.float32

    def call(kernel, name, operands, places, shapes, scratch, out_place=VMEM):
        return pl.pallas_call(
            kernel,
            out_shape=[jax.ShapeDtypeStruct(shape, f32) for shape in shapes],
            in_specs=places,
            out_specs=[out_place] * len(shapes),
            scratch_shapes=scratch,
            compiler_params=PARAMS,
            name=name,
        )(*operands)

    def around(pieces):
        return [pieces[0]] + [
            lax.ppermute(pieces[k], "slab", [(i, (i + k) % slabs) for i in range(slabs)])
            for k in range(1, slabs)
        ]

    def beside(first, last):
        up = [(i + 1, i) for i in range(tiles - 1)]
        down = [(i, i + 1) for i in range(tiles - 1)]
        return lax.ppermute(first, "tile", up), lax.ppermute(last, "tile", down)

    dma = pltpu.SemaphoreType.DMA
    pieces = call(
        slow_kernel, "slow", (slowness,), [HBM], [(ROWS, WIDE)] * DEPTHS,
        [pltpu.VMEM((ROWS, GRID), f32), dma],
    )
    pieces = around(pieces)
    head, tail = call(
        wave_kernel, "wave", (wavefield,), [HBM], [(HALO, COMPS, WIDE)] * 2,
        [
            pltpu.VMEM((FREQS, 2, ROWS, COLS), f32),
            pltpu.VMEM((2, FREQS, 2, ROWS, LANES), f32),
            pltpu.VMEM((ROWS * COMPS, WIDE), f32),
            dma((3,)),
        ],
    )
    below, above = beside(head, tail)
    edge_rows = sum(ROWS - 8 * depth for depth in range(DEPTHS))
    own, first, last = call(
        edge_kernel, "edges", pieces, [VMEM] * DEPTHS,
        [(DEPTHS, ROWS, WIDE)] + [(edge_rows, WIDE)] * 2,
        [pltpu.VMEM((DEPTHS * ROWS, WIDE), f32)],
    )
    edge_below, edge_above = beside(first, last)
    images = call(
        main_kernel, "migrate",
        (head, tail, above, below, own, edge_above, edge_below, angular_freq, filter_taps.reshape(-1)),
        [ANY] * 7 + [SMEM] * 2, [(ROWS, COLS)] * DEPTHS, SCRATCH,
    )
    return call(
        join_kernel, "join", around(images), [ANY] * DEPTHS, [(1, ROWS, GRID)], [dma((DEPTHS,))], ANY
    )[0]


def solution(mesh):
    placed = (P(None, None, "tile", None), P("slab", "tile", None), P(), P())
    return jax.shard_map(
        local, mesh=mesh, in_specs=placed, out_specs=P("slab", "tile", None), check_vma=False
    )
```

```python
import math

import jax
import jax.numpy as jnp
import numpy as np
from jax import lax
from jax.experimental import pallas as pl
from jax.experimental.pallas import tpu as pltpu
from jax.sharding import PartitionSpec as P

TERMS = 8
DEPTHS = 4
FREQS = 4
LANES = 128
COMPS = 2 * FREQS
HALO = DEPTHS * (TERMS - 1)
ROWS = 32
SPAN = 3 * ROWS
GRID = 2048
COLS = 512
WIDE = COLS + LANES
MOST = 32
FINISH = 8
SPREAD = 8
VMEM = pl.BlockSpec(memory_space=pltpu.VMEM)
ANY = pl.BlockSpec(memory_space=pl.ANY)
HBM = pl.BlockSpec(memory_space=pltpu.HBM)
SMEM = pl.BlockSpec(memory_space=pltpu.SMEM)
PARAMS = pltpu.CompilerParams(vmem_limit_bytes=48 * 1024 * 1024)

SCRATCH = [
    pltpu.VMEM((DEPTHS, SPAN, WIDE), jnp.float32),
    pltpu.VMEM((SPAN, COMPS, WIDE), jnp.float32),
    pltpu.VMEM((DEPTHS * ROWS, WIDE), jnp.float32),
    pltpu.VMEM((DEPTHS, ROWS, COLS), jnp.float32),
    pltpu.VMEM((2 * TERMS, COMPS, LANES), jnp.float32),
] + [pltpu.VMEM((SPAN, COMPS, WIDE), jnp.float32)] * TERMS


def fit(function, low, high, count):
    angle = (np.arange(400) + 0.5) * np.pi / 400
    q = 0.5 * (low + high) + 0.5 * (high - low) * np.cos(angle)
    rows = np.stack([q**power for power in range(count)], 1)
    return np.linalg.lstsq(rows, function(q), rcond=None)[0]


COEFFICIENTS = 6
ARGUMENT_LIMIT = 1.5
SINE = fit(lambda q: np.sin(np.sqrt(q)) / np.sqrt(q), 0.0, ARGUMENT_LIMIT**2, COEFFICIENTS)
COSINE = fit(lambda q: np.cos(np.sqrt(q)), 0.0, ARGUMENT_LIMIT**2, COEFFICIENTS)


def edge_columns(right, left, block):
    right = jnp.where(block < GRID // COLS - 1, right, 0.0)
    left = jnp.where(block > 0, left, 0.0)
    lane = lax.broadcasted_iota(jnp.int32, right.shape, right.ndim - 1)
    return jnp.where(lane < LANES // 2, right, left)


def edge_starts(block):
    right = jnp.minimum(block + 1, GRID // COLS - 1) * COLS
    left = jnp.maximum(block * COLS - LANES, 0)
    return pl.multiple_of(right, LANES), pl.multiple_of(left, LANES)


def shuffle(column_axis):
    vectors = WIDE // LANES
    column = lax.broadcasted_iota(jnp.int32, (WIDE, WIDE), column_axis)
    place = lax.broadcasted_iota(jnp.int32, (WIDE, WIDE), 1 - column_axis)
    lane = place & (LANES - 1)
    here = lane * vectors + (place >> 7)
    return jnp.where(column == here, 1.0, 0.0).astype(jnp.bfloat16)


def exact_dot(rows, matrix):
    high = rows.astype(jnp.bfloat16)
    rest = rows - high.astype(jnp.float32)
    middle = rest.astype(jnp.bfloat16)
    low = (rest - middle.astype(jnp.float32)).astype(jnp.bfloat16)
    dots = [jnp.dot(part, matrix, preferred_element_type=jnp.float32) for part in (high, middle, low)]
    return (dots[0] + dots[1]) + dots[2]


def slow_kernel(slow_ref, *refs):
    pieces, (held, sem) = refs[:DEPTHS], refs[DEPTHS:]
    here = lax.axis_index("slab")
    copy = pltpu.make_async_copy(slow_ref.at[0], held, sem)
    copy.start()
    copy.wait()
    for shift, out in enumerate(pieces):
        block = lax.rem(here + shift, DEPTHS)
        right, left = edge_starts(block)
        out[:, :COLS] = held[:, pl.ds(pl.multiple_of(block * COLS, COLS), COLS)]
        out[:, COLS:] = edge_columns(held[:, pl.ds(right, LANES)], held[:, pl.ds(left, LANES)], block)


def wave_kernel(wave_ref, head_ref, tail_ref, held, edges, lined, sems):
    here = lax.axis_index("slab")
    right, left = edge_starts(here)
    start = pl.multiple_of(here * COLS, COLS)
    copies = [
        pltpu.make_async_copy(wave_ref.at[:, :, :, pl.ds(start, COLS)], held, sems.at[0]),
        pltpu.make_async_copy(wave_ref.at[:, :, :, pl.ds(right, LANES)], edges.at[0], sems.at[1]),
        pltpu.make_async_copy(wave_ref.at[:, :, :, pl.ds(left, LANES)], edges.at[1], sems.at[2]),
    ]
    for copy in copies:
        copy.start()
    matrix = shuffle(0)
    for copy in copies:
        copy.wait()
    for group in range(ROWS // 8):
        rows = slice(group * 8, group * 8 + 8)
        for piece in range(WIDE // LANES):
            lanes = slice(piece * LANES, (piece + 1) * LANES)
            parts = []
            for comp in range(2):
                for freq in range(FREQS):
                    if piece < COLS // LANES:
                        parts.append(held[freq, comp, rows, lanes])
                    else:
                        parts.append(
                            edge_columns(edges[0, freq, comp, rows], edges[1, freq, comp, rows], here)
                        )
            turned = jnp.swapaxes(jnp.stack(parts), 0, 1).reshape(8 * COMPS, LANES)
            low = group * 8 * COMPS
            lined[low : low + 8 * COMPS, lanes] = turned
    field = exact_dot(lined[...], matrix).reshape(ROWS, COMPS, WIDE)
    head_ref[...] = field[:HALO]
    tail_ref[...] = field[ROWS - HALO :]


def edge_kernel(*refs):
    pieces, (own_ref, first_ref, last_ref, lined) = refs[:DEPTHS], refs[DEPTHS:]
    here = lax.axis_index("slab")
    for shift, piece in enumerate(pieces):
        depth = lax.rem(here - shift + DEPTHS, DEPTHS)
        lined[pl.ds(pl.multiple_of(depth * ROWS, ROWS), ROWS)] = piece[...]
    own = exact_dot(lined[...], shuffle(0)).reshape(DEPTHS, ROWS, WIDE)
    own_ref[...] = own
    low = 0
    for depth in range(DEPTHS):
        count = ROWS - 8 * depth
        first_ref[low : low + count] = own[depth, :count]
        last_ref[low : low + count] = own[depth, ROWS - count :]
        low += count


def block_rows(count):
    return min(range(8, MOST + 1), key=lambda size: -(-count // size) * (size + 8))


def main_kernel(
    head, tail, above, below, own, edge_above, edge_below, omega_ref, taps_ref, *refs
):
    images, (slow, wide, mixed, held, taps, *terms) = refs[:DEPTHS], refs[DEPTHS:]
    here = lax.axis_index("slab")
    begin = ROWS - HALO
    terms[0][begin:ROWS] = above[...]
    terms[0][ROWS : ROWS + HALO] = head[...]
    terms[0][ROWS + HALO : 2 * ROWS] = tail[HALO - begin :]
    terms[0][2 * ROWS : 2 * ROWS + HALO] = below[...]
    slow[:, ROWS : 2 * ROWS] = own[...]
    low = 0
    for depth in range(DEPTHS):
        count = ROWS - 8 * depth
        slow[depth, ROWS - count : ROWS] = edge_above[low : low + count]
        slow[depth, 2 * ROWS : 2 * ROWS + count] = edge_below[low : low + count]
        low += count
    matrix = shuffle(1)[:, :COLS]
    sublane = lax.broadcasted_iota(jnp.int32, (COMPS, LANES), 0)
    real = sublane < FREQS

    def of_frequency(value):
        vector = jnp.full((COMPS, LANES), value(FREQS - 1), jnp.float32)
        for freq in range(FREQS - 1):
            vector = jnp.where((sublane & (FREQS - 1)) == freq, value(freq), vector)
        return vector

    def tap(part, order):
        return of_frequency(lambda freq: taps_ref[freq, order, part])

    omega = of_frequency(lambda freq: 0.5 * omega_ref[freq])
    straight_taps = [tap(0, order) for order in range(TERMS)]
    crossed_taps = [jnp.where(real, tap(1, order), -tap(1, order)) for order in range(TERMS)]
    for order in range(TERMS):
        taps[order] = straight_taps[order]
        taps[TERMS + order] = crossed_taps[order]

    def coefficient(index):
        return jnp.where(real, -float(SINE[index]), float(COSINE[index])).astype(jnp.float32)

    def rows_loop(low, high, size, body):
        full = (high - low) // size

        def step(index, carry):
            body(low + index * size, size)
            return carry

        lax.fori_loop(0, full, step, 0)
        if (high - low) % size:
            body(low + full * size, (high - low) % size)

    def covering_loop(low, high, size, body):

        def step(index, carry):
            body(jnp.minimum(low + index * size, high - size), size)
            return carry

        lax.fori_loop(0, -(-(high - low) // size), step, 0)

    for depth in range(DEPTHS):
        reach = HALO - depth * (TERMS - 1)
        lower, upper = ROWS - reach, 2 * ROWS + reach

        def spread(start, count):
            for row in range(count):
                line = slow[depth, pl.ds(start + row, 1), :] * 2.0
                wide[start + row] = jnp.broadcast_to(line, (COMPS, WIDE))

        covering_loop(lower + 1, upper - 1, SPREAD, spread)
        for order in range(1, TERMS):

            def apply(start, count):
                pieces = range(WIDE // LANES)

                def load(ref, at):
                    return [ref[at, :, p * LANES : (p + 1) * LANES] for p in pieces]

                here_row = load(terms[order - 1], start)
                pair = [a + b for a, b in zip(load(terms[order - 1], start - 1), here_row)]
                for row in range(count):
                    next_row = load(terms[order - 1], start + row + 1)
                    next_pair = [a + b for a, b in zip(here_row, next_row)]
                    tall = [a + b for a, b in zip(pair, next_pair)]
                    before = pltpu.roll(tall[-1], 1, 1)
                    after = pltpu.roll(tall[0], LANES - 1, 1)
                    chain = [before] + tall + [after]
                    sums = [a + b for a, b in zip(chain[:-1], chain[1:])]
                    full = [a + b for a, b in zip(sums[:-1], sums[1:])]
                    for p in pieces:
                        lanes = slice(p * LANES, (p + 1) * LANES)
                        fresh = wide[start + row, :, lanes] * (0.125 * full[p] - here_row[p])
                        if order == 1:
                            fresh = 0.5 * fresh
                        else:
                            fresh = fresh - terms[order - 2][start + row, :, lanes]
                        terms[order][start + row, :, lanes] = fresh
                    here_row, pair = next_row, next_pair

            covering_loop(lower + order, upper - order, block_rows(upper - lower - 2 * order), apply)

        def finish(start, count):
            rows = range(count)
            for piece in range(WIDE // LANES):
                lanes = slice(piece * LANES, (piece + 1) * LANES)
                straight, crossed = [None] * count, [None] * count
                for order in range(TERMS):
                    one, other = taps[order], taps[TERMS + order]
                    for row in rows:
                        term = terms[order][start + row, :, lanes]
                        along, across = one * term, other * term
                        straight[row] = along if order == 0 else straight[row] + along
                        crossed[row] = across if order == 0 else crossed[row] + across
                offsets = [omega * wide[start + row, :, lanes] - math.pi / 2 for row in rows]
                squares = [offset * offset for offset in offsets]
                polys = [coefficient(COEFFICIENTS - 1)] * count
                for index in range(COEFFICIENTS - 2, -1, -1):
                    polys = [poly * square + coefficient(index) for poly, square in zip(polys, squares)]
                for row in rows:
                    filtered = straight[row] + pltpu.roll(crossed[row], FREQS, 0)
                    own = polys[row] * jnp.where(real, offsets[row], 1.0)
                    other = pltpu.roll(own, FREQS, 0)
                    cosine = jnp.where(real, own, other)
                    sine = jnp.where(real, -other, own)
                    terms[0][start + row, :, lanes] = (
                        filtered * cosine + pltpu.roll(filtered, FREQS, 0) * sine
                    )

        rows_loop(lower + TERMS - 1, upper - TERMS + 1, FINISH, finish)

        def gather(index, carry):
            start = pl.multiple_of(index * 8, 8)
            block = terms[0][pl.ds(ROWS + start, 8)]
            mixed[pl.ds(depth * ROWS + start, 8)] = jnp.sum(block[:, :FREQS], axis=1)
            return carry

        lax.fori_loop(0, ROWS // 8, gather, 0)
    held[...] = exact_dot(mixed[...], matrix).reshape(held.shape)
    for shift, image in enumerate(images):
        image[...] = held[lax.rem(here + shift, DEPTHS)]


def join_kernel(*refs):
    pieces, (out, sems) = refs[:DEPTHS], refs[DEPTHS:]
    here = lax.axis_index("slab")
    copies = []
    for shift, piece in enumerate(pieces):
        block = lax.rem(here - shift + DEPTHS, DEPTHS)
        columns = pl.ds(pl.multiple_of(block * COLS, COLS), COLS)
        copies.append(pltpu.make_async_copy(piece, out.at[0, :, columns], sems.at[shift]))
        copies[-1].start()
    for copy in copies:
        copy.wait()


def local(wavefield, slowness, angular_freq, filter_taps):
    tiles, slabs = lax.axis_size("tile"), lax.axis_size("slab")
    f32 = jnp.float32

    def call(kernel, name, operands, places, shapes, scratch, out_place=VMEM):
        return pl.pallas_call(
            kernel,
            out_shape=[jax.ShapeDtypeStruct(shape, f32) for shape in shapes],
            in_specs=places,
            out_specs=[out_place] * len(shapes),
            scratch_shapes=scratch,
            compiler_params=PARAMS,
            name=name,
        )(*operands)

    def around(pieces):
        return [pieces[0]] + [
            lax.ppermute(pieces[k], "slab", [(i, (i + k) % slabs) for i in range(slabs)])
            for k in range(1, slabs)
        ]

    def beside(first, last):
        up = [(i + 1, i) for i in range(tiles - 1)]
        down = [(i, i + 1) for i in range(tiles - 1)]
        return lax.ppermute(first, "tile", up), lax.ppermute(last, "tile", down)

    dma = pltpu.SemaphoreType.DMA
    pieces = call(
        slow_kernel, "slow", (slowness,), [HBM], [(ROWS, WIDE)] * DEPTHS,
        [pltpu.VMEM((ROWS, GRID), f32), dma],
    )
    pieces = around(pieces)
    head, tail = call(
        wave_kernel, "wave", (wavefield,), [HBM], [(HALO, COMPS, WIDE)] * 2,
        [
            pltpu.VMEM((FREQS, 2, ROWS, COLS), f32),
            pltpu.VMEM((2, FREQS, 2, ROWS, LANES), f32),
            pltpu.VMEM((ROWS * COMPS, WIDE), f32),
            dma((3,)),
        ],
    )
    below, above = beside(head, tail)
    edge_rows = sum(ROWS - 8 * depth for depth in range(DEPTHS))
    own, first, last = call(
        edge_kernel, "edges", pieces, [VMEM] * DEPTHS,
        [(DEPTHS, ROWS, WIDE)] + [(edge_rows, WIDE)] * 2,
        [pltpu.VMEM((DEPTHS * ROWS, WIDE), f32)],
    )
    edge_below, edge_above = beside(first, last)
    images = call(
        main_kernel, "migrate",
        (head, tail, above, below, own, edge_above, edge_below, angular_freq, filter_taps),
        [VMEM] * 7 + [SMEM] * 2, [(ROWS, COLS)] * DEPTHS, SCRATCH,
    )
    return call(
        join_kernel, "join", around(images), [ANY] * DEPTHS, [(1, ROWS, GRID)], [dma((DEPTHS,))], ANY
    )[0]


def solution(mesh):
    placed = (P(None, None, "tile", None), P("slab", "tile", None), P(), P())
    return jax.shard_map(
        local, mesh=mesh, in_specs=placed, out_specs=P("slab", "tile", None), check_vma=False
    )
```

```python
import math

import jax
import jax.numpy as jnp
import numpy as np
from jax import lax
from jax.experimental import pallas as pl
from jax.experimental.pallas import tpu as pltpu
from jax.sharding import PartitionSpec as P

TERMS = 8
DEPTHS = 4
FREQS = 4
LANES = 128
COMPS = 2 * FREQS
HALO = DEPTHS * (TERMS - 1)
ROWS = 32
SPAN = 3 * ROWS
GRID = 2048
COLS = 512
WIDE = COLS + LANES
MOST = 32
FINISH = 8
SPREAD = 8
VMEM = pl.BlockSpec(memory_space=pltpu.VMEM)
ANY = pl.BlockSpec(memory_space=pl.ANY)
HBM = pl.BlockSpec(memory_space=pltpu.HBM)
SMEM = pl.BlockSpec(memory_space=pltpu.SMEM)
PARAMS = pltpu.CompilerParams(vmem_limit_bytes=48 * 1024 * 1024)

SCRATCH = [
    pltpu.VMEM((DEPTHS, SPAN, WIDE), jnp.float32),
    pltpu.VMEM((SPAN, COMPS, WIDE), jnp.float32),
    pltpu.VMEM((DEPTHS * ROWS, WIDE), jnp.float32),
    pltpu.VMEM((DEPTHS, ROWS, COLS), jnp.float32),
    pltpu.VMEM((2 * TERMS, COMPS, LANES), jnp.float32),
] + [pltpu.VMEM((SPAN, COMPS, WIDE), jnp.float32)] * TERMS


def fit(function, low, high, count):
    angle = (np.arange(400) + 0.5) * np.pi / 400
    q = 0.5 * (low + high) + 0.5 * (high - low) * np.cos(angle)
    rows = np.stack([q**power for power in range(count)], 1)
    return np.linalg.lstsq(rows, function(q), rcond=None)[0]


COEFFICIENTS = 5
ARGUMENT_LIMIT = 1.5
SINE = fit(lambda q: np.sin(np.sqrt(q)) / np.sqrt(q), 0.0, ARGUMENT_LIMIT**2, COEFFICIENTS)
COSINE = fit(lambda q: np.cos(np.sqrt(q)), 0.0, ARGUMENT_LIMIT**2, COEFFICIENTS)


def edge_columns(right, left, block):
    right = jnp.where(block < GRID // COLS - 1, right, 0.0)
    left = jnp.where(block > 0, left, 0.0)
    lane = lax.broadcasted_iota(jnp.int32, right.shape, right.ndim - 1)
    return jnp.where(lane < LANES // 2, right, left)


def edge_starts(block):
    right = jnp.minimum(block + 1, GRID // COLS - 1) * COLS
    left = jnp.maximum(block * COLS - LANES, 0)
    return pl.multiple_of(right, LANES), pl.multiple_of(left, LANES)


def shuffle(column_axis):
    vectors = WIDE // LANES
    column = lax.broadcasted_iota(jnp.int32, (WIDE, WIDE), column_axis)
    place = lax.broadcasted_iota(jnp.int32, (WIDE, WIDE), 1 - column_axis)
    lane = place & (LANES - 1)
    here = lane * vectors + (place >> 7)
    return jnp.where(column == here, 1.0, 0.0).astype(jnp.bfloat16)


def exact_dot(rows, matrix):
    high = rows.astype(jnp.bfloat16)
    rest = rows - high.astype(jnp.float32)
    middle = rest.astype(jnp.bfloat16)
    low = (rest - middle.astype(jnp.float32)).astype(jnp.bfloat16)
    dots = [jnp.dot(part, matrix, preferred_element_type=jnp.float32) for part in (high, middle, low)]
    return (dots[0] + dots[1]) + dots[2]


def slow_kernel(slow_ref, *refs):
    pieces, (held, sem) = refs[:DEPTHS], refs[DEPTHS:]
    here = lax.axis_index("slab")
    copy = pltpu.make_async_copy(slow_ref.at[0], held, sem)
    copy.start()
    copy.wait()
    for shift, out in enumerate(pieces):
        block = lax.rem(here + shift, DEPTHS)
        right, left = edge_starts(block)
        out[:, :COLS] = held[:, pl.ds(pl.multiple_of(block * COLS, COLS), COLS)]
        out[:, COLS:] = edge_columns(held[:, pl.ds(right, LANES)], held[:, pl.ds(left, LANES)], block)


def wave_kernel(wave_ref, head_ref, tail_ref, held, edges, lined, sems):
    here = lax.axis_index("slab")
    right, left = edge_starts(here)
    start = pl.multiple_of(here * COLS, COLS)
    copies = [
        pltpu.make_async_copy(wave_ref.at[:, :, :, pl.ds(start, COLS)], held, sems.at[0]),
        pltpu.make_async_copy(wave_ref.at[:, :, :, pl.ds(right, LANES)], edges.at[0], sems.at[1]),
        pltpu.make_async_copy(wave_ref.at[:, :, :, pl.ds(left, LANES)], edges.at[1], sems.at[2]),
    ]
    for copy in copies:
        copy.start()
    matrix = shuffle(0)
    for copy in copies:
        copy.wait()
    for group in range(ROWS // 8):
        rows = slice(group * 8, group * 8 + 8)
        for piece in range(WIDE // LANES):
            lanes = slice(piece * LANES, (piece + 1) * LANES)
            parts = []
            for comp in range(2):
                for freq in range(FREQS):
                    if piece < COLS // LANES:
                        parts.append(held[freq, comp, rows, lanes])
                    else:
                        parts.append(
                            edge_columns(edges[0, freq, comp, rows], edges[1, freq, comp, rows], here)
                        )
            turned = jnp.swapaxes(jnp.stack(parts), 0, 1).reshape(8 * COMPS, LANES)
            low = group * 8 * COMPS
            lined[low : low + 8 * COMPS, lanes] = turned
    field = exact_dot(lined[...], matrix).reshape(ROWS, COMPS, WIDE)
    head_ref[...] = field[:HALO]
    tail_ref[...] = field[ROWS - HALO :]


def edge_kernel(*refs):
    pieces, (own_ref, first_ref, last_ref, lined) = refs[:DEPTHS], refs[DEPTHS:]
    here = lax.axis_index("slab")
    for shift, piece in enumerate(pieces):
        depth = lax.rem(here - shift + DEPTHS, DEPTHS)
        lined[pl.ds(pl.multiple_of(depth * ROWS, ROWS), ROWS)] = piece[...]
    own = exact_dot(lined[...], shuffle(0)).reshape(DEPTHS, ROWS, WIDE)
    own_ref[...] = own
    low = 0
    for depth in range(DEPTHS):
        count = ROWS - 8 * depth
        first_ref[low : low + count] = own[depth, :count]
        last_ref[low : low + count] = own[depth, ROWS - count :]
        low += count


def block_rows(count):
    return min(range(8, MOST + 1), key=lambda size: -(-count // size) * (size + 8))


def main_kernel(
    head, tail, above, below, own, edge_above, edge_below, omega_ref, taps_ref, *refs
):
    images, (slow, wide, mixed, held, taps, *terms) = refs[:DEPTHS], refs[DEPTHS:]
    here = lax.axis_index("slab")
    begin = ROWS - HALO
    terms[0][begin:ROWS] = above[...]
    terms[0][ROWS : ROWS + HALO] = head[...]
    terms[0][ROWS + HALO : 2 * ROWS] = tail[HALO - begin :]
    terms[0][2 * ROWS : 2 * ROWS + HALO] = below[...]
    slow[:, ROWS : 2 * ROWS] = own[...]
    low = 0
    for depth in range(DEPTHS):
        count = ROWS - 8 * depth
        slow[depth, ROWS - count : ROWS] = edge_above[low : low + count]
        slow[depth, 2 * ROWS : 2 * ROWS + count] = edge_below[low : low + count]
        low += count
    matrix = shuffle(1)[:, :COLS]
    sublane = lax.broadcasted_iota(jnp.int32, (COMPS, LANES), 0)
    real = sublane < FREQS

    def of_frequency(value):
        vector = jnp.full((COMPS, LANES), value(FREQS - 1), jnp.float32)
        for freq in range(FREQS - 1):
            vector = jnp.where((sublane & (FREQS - 1)) == freq, value(freq), vector)
        return vector

    def tap(part, order):
        return of_frequency(lambda freq: taps_ref[freq, order, part])

    omega = of_frequency(lambda freq: 0.5 * omega_ref[freq])
    straight_taps = [tap(0, order) for order in range(TERMS)]
    crossed_taps = [jnp.where(real, tap(1, order), -tap(1, order)) for order in range(TERMS)]
    for order in range(TERMS):
        taps[order] = straight_taps[order]
        taps[TERMS + order] = crossed_taps[order]

    def coefficient(index):
        return jnp.where(real, -float(SINE[index]), float(COSINE[index])).astype(jnp.float32)

    def rows_loop(low, high, size, body):
        full = (high - low) // size

        def step(index, carry):
            body(low + index * size, size)
            return carry

        lax.fori_loop(0, full, step, 0)
        if (high - low) % size:
            body(low + full * size, (high - low) % size)

    def covering_loop(low, high, size, body):

        def step(index, carry):
            body(jnp.minimum(low + index * size, high - size), size)
            return carry

        lax.fori_loop(0, -(-(high - low) // size), step, 0)

    for depth in range(DEPTHS):
        reach = HALO - depth * (TERMS - 1)
        lower, upper = ROWS - reach, 2 * ROWS + reach

        def spread(start, count):
            for row in range(count):
                line = slow[depth, pl.ds(start + row, 1), :] * 2.0
                wide[start + row] = jnp.broadcast_to(line, (COMPS, WIDE))

        covering_loop(lower + 1, upper - 1, SPREAD, spread)
        for order in range(1, TERMS):

            def apply(start, count):
                pieces = range(WIDE // LANES)

                def load(ref, at):
                    return [ref[at, :, p * LANES : (p + 1) * LANES] for p in pieces]

                here_row = load(terms[order - 1], start)
                pair = [a + b for a, b in zip(load(terms[order - 1], start - 1), here_row)]
                for row in range(count):
                    next_row = load(terms[order - 1], start + row + 1)
                    next_pair = [a + b for a, b in zip(here_row, next_row)]
                    tall = [a + b for a, b in zip(pair, next_pair)]
                    before = pltpu.roll(tall[-1], 1, 1)
                    after = pltpu.roll(tall[0], LANES - 1, 1)
                    chain = [before] + tall + [after]
                    sums = [a + b for a, b in zip(chain[:-1], chain[1:])]
                    full = [a + b for a, b in zip(sums[:-1], sums[1:])]
                    for p in pieces:
                        lanes = slice(p * LANES, (p + 1) * LANES)
                        fresh = wide[start + row, :, lanes] * (0.125 * full[p] - here_row[p])
                        if order == 1:
                            fresh = 0.5 * fresh
                        else:
                            fresh = fresh - terms[order - 2][start + row, :, lanes]
                        terms[order][start + row, :, lanes] = fresh
                    here_row, pair = next_row, next_pair

            covering_loop(lower + order, upper - order, block_rows(upper - lower - 2 * order), apply)

        def finish(start, count):
            rows = range(count)
            for piece in range(WIDE // LANES):
                lanes = slice(piece * LANES, (piece + 1) * LANES)
                straight, crossed = [None] * count, [None] * count
                for order in range(TERMS):
                    one, other = taps[order], taps[TERMS + order]
                    for row in rows:
                        term = terms[order][start + row, :, lanes]
                        along, across = one * term, other * term
                        straight[row] = along if order == 0 else straight[row] + along
                        crossed[row] = across if order == 0 else crossed[row] + across
                offsets = [omega * wide[start + row, :, lanes] - math.pi / 2 for row in rows]
                squares = [offset * offset for offset in offsets]
                polys = [coefficient(COEFFICIENTS - 1)] * count
                for index in range(COEFFICIENTS - 2, -1, -1):
                    polys = [poly * square + coefficient(index) for poly, square in zip(polys, squares)]
                for row in rows:
                    filtered = straight[row] + pltpu.roll(crossed[row], FREQS, 0)
                    own = polys[row] * jnp.where(real, offsets[row], 1.0)
                    other = pltpu.roll(own, FREQS, 0)
                    cosine = jnp.where(real, own, other)
                    sine = jnp.where(real, -other, own)
                    terms[0][start + row, :, lanes] = (
                        filtered * cosine + pltpu.roll(filtered, FREQS, 0) * sine
                    )

        rows_loop(lower + TERMS - 1, upper - TERMS + 1, FINISH, finish)

        block = terms[0][ROWS : 2 * ROWS, :FREQS]
        mixed[depth * ROWS : (depth + 1) * ROWS] = jnp.sum(block, axis=1)
    held[...] = exact_dot(mixed[...], matrix).reshape(held.shape)
    for shift, image in enumerate(images):
        image[...] = held[lax.rem(here + shift, DEPTHS)]


def join_kernel(*refs):
    pieces, (out, sems) = refs[:DEPTHS], refs[DEPTHS:]
    here = lax.axis_index("slab")
    copies = []
    for shift, piece in enumerate(pieces):
        block = lax.rem(here - shift + DEPTHS, DEPTHS)
        columns = pl.ds(pl.multiple_of(block * COLS, COLS), COLS)
        copies.append(pltpu.make_async_copy(piece, out.at[0, :, columns], sems.at[shift]))
        copies[-1].start()
    for copy in copies:
        copy.wait()


def local(wavefield, slowness, angular_freq, filter_taps):
    tiles, slabs = lax.axis_size("tile"), lax.axis_size("slab")
    f32 = jnp.float32

    def call(kernel, name, operands, places, shapes, scratch, out_place=VMEM):
        return pl.pallas_call(
            kernel,
            out_shape=[jax.ShapeDtypeStruct(shape, f32) for shape in shapes],
            in_specs=places,
            out_specs=[out_place] * len(shapes),
            scratch_shapes=scratch,
            compiler_params=PARAMS,
            name=name,
        )(*operands)

    def around(pieces):
        return [pieces[0]] + [
            lax.ppermute(pieces[k], "slab", [(i, (i + k) % slabs) for i in range(slabs)])
            for k in range(1, slabs)
        ]

    def beside(first, last):
        up = [(i + 1, i) for i in range(tiles - 1)]
        down = [(i, i + 1) for i in range(tiles - 1)]
        return lax.ppermute(first, "tile", up), lax.ppermute(last, "tile", down)

    dma = pltpu.SemaphoreType.DMA
    pieces = call(
        slow_kernel, "slow", (slowness,), [HBM], [(ROWS, WIDE)] * DEPTHS,
        [pltpu.VMEM((ROWS, GRID), f32), dma],
    )
    pieces = around(pieces)
    head, tail = call(
        wave_kernel, "wave", (wavefield,), [HBM], [(HALO, COMPS, WIDE)] * 2,
        [
            pltpu.VMEM((FREQS, 2, ROWS, COLS), f32),
            pltpu.VMEM((2, FREQS, 2, ROWS, LANES), f32),
            pltpu.VMEM((ROWS * COMPS, WIDE), f32),
            dma((3,)),
        ],
    )
    below, above = beside(head, tail)
    edge_rows = sum(ROWS - 8 * depth for depth in range(DEPTHS))
    own, first, last = call(
        edge_kernel, "edges", pieces, [VMEM] * DEPTHS,
        [(DEPTHS, ROWS, WIDE)] + [(edge_rows, WIDE)] * 2,
        [pltpu.VMEM((DEPTHS * ROWS, WIDE), f32)],
    )
    edge_below, edge_above = beside(first, last)
    images = call(
        main_kernel, "migrate",
        (head, tail, above, below, own, edge_above, edge_below, angular_freq, filter_taps),
        [VMEM] * 7 + [SMEM] * 2, [(ROWS, COLS)] * DEPTHS, SCRATCH,
    )
    return call(
        join_kernel, "join", around(images), [ANY] * DEPTHS, [(1, ROWS, GRID)], [dma((DEPTHS,))], ANY
    )[0]


def solution(mesh):
    placed = (P(None, None, "tile", None), P("slab", "tile", None), P(), P())
    return jax.shard_map(
        local, mesh=mesh, in_specs=placed, out_specs=P("slab", "tile", None), check_vma=False
    )
```
